32 devices in a mesh: phase: 4 (over x, core), ctx: 2 (over y), tp: 4 (over z).
Axes of the slice: x: 2, y: 2, z: 4, core: 2. Of those that a mesh axis runs over, the one named last changes fastest.
Arguments:
- queries: bfloat16 [4, 256, 4096], P('phase', 'ctx', 'tp'), may hold values from -8 to 8
- keys: bfloat16 [4, 256, 512], P('phase', 'ctx', 'tp'), may hold values from -8 to 8
- values: bfloat16 [4, 256, 512], P('phase', 'ctx', 'tp'), may hold values from -6 to 6
- seg_ids: int32 [4, 256], P('phase'), may hold values from 0 to 3, never falling along the last dimension, each value on 1 to 128 neighbouring positions
- out_weight: bfloat16 [4096, 8192], P('tp', 'ctx'), may hold values from -0.5 to 0.5
- embedded: bfloat16 [256, 8192], P('tp', 'ctx'), may hold values from -6 to 6
- hidden_prev: bfloat16 [4, 256, 8192], P('phase', 'tp', 'ctx'), may hold values from -6 to 6
Outputs:
- hidden_next: bfloat16 [4, 256, 8192], P('phase', 'tp', 'ctx')
The draws below stay inside these ranges and needn't reach their ends.
Inputs may be any that keep to these rules, and one draw needn't show every extreme that they name: `seg_ids`: within each section the segment number never falls; a segment holds at most 128 tokens.
All inputs are finite; a program needn't handle non-finite values.
Results may differ from the reference program's by a relative error of at most 0.015.
Values may be sent and summed in bfloat16 or wider, within the bound.
No kernel may reach another device: no remote copies, remote signals or barrier semaphores. Data moves between devices by JAX's collectives and lax.ppermute only.
A program may use at most 64 MiB of HBM per device.

```python
import math
import jax
import jax.numpy as jnp
import numpy as np
from jax import lax

D = 8192
HEADS = 32
KV_HEADS = 4
HEAD_DIM = 128
SEGS = 4
S_SEC = 256
SECTIONS = 4
SEG_MOST = 128
N_TP = 4


def base_block(key, salt, width):
    return jnp.clip(jax.random.normal(jax.random.fold_in(key, salt), (SECTIONS, S_SEC, width), jnp.float32), -8.0, 8.0)


def draw_queries(key, part):
    result = base_block(key, 1, HEADS * HEAD_DIM)
    return result.astype(jnp.bfloat16)


def draw_keys(key, part):
    result = base_block(key, 2, KV_HEADS * HEAD_DIM)
    return result.astype(jnp.bfloat16)


def block_levels(key, shape, shards, smallest, top_value):
    def one(axis_at, blocks):
        heights = jax.random.uniform(jax.random.fold_in(jax.random.fold_in(key, 6), axis_at), (blocks,), jnp.float32, smallest / len(shards), top_value / len(shards))
        return jnp.repeat(jnp.exp(heights), shape[axis_at] // blocks).reshape((-1,) + (1,) * (len(shape) - axis_at - 1))

    loudness = one(*shards[0])
    for cut in shards[1:]:
        loudness = loudness * one(*cut)
    return loudness


def length_profile(number_of, total, bound, lean):
    portions = [(1 << 20) // math.isqrt(standing ** lean) + 1 for standing in range(2, number_of + 1)]
    surplus, given = total - bound - (number_of - 1), [1] * (number_of - 1)
    while surplus > 0:
        movable = [i for i in range(number_of - 1) if given[i] < bound]
        mass, remaining = sum([portions[i] for i in movable]), surplus
        for i in movable:
            extra = min(bound - given[i], max(1, remaining * portions[i] // mass), surplus)
            given[i] = given[i] + extra
            surplus = surplus - extra
    return np.array([bound] + given)


def ragged_sizes(rng, count, total, most, slope):
    if count == 2:
        one = jax.random.randint(rng, (), max(1, total - most), min(most, total - 1) + 1)
        return jnp.stack([one, total - one])
    lengths = jnp.asarray(length_profile(count, total, most, slope), jnp.int32)
    twos = (count - 1) // 2
    giver, receiver = lengths[1:1 + 2 * twos:2], lengths[2:2 + 2 * twos:2]
    margin = jnp.minimum(giver - 1, most - receiver)
    passed = jax.random.randint(jax.random.fold_in(rng, 1), (twos,), 0, 1 << 20) % (margin + 1)
    lengths = lengths.at[1:1 + 2 * twos:2].set(giver - passed).at[2:2 + 2 * twos:2].set(receiver + passed)
    return lengths[jax.random.permutation(jax.random.fold_in(rng, 2), count)]


def noise(rng, extent, scale, limit, cuts=(), kind=jnp.bfloat16):
    factor_of = block_levels(rng, extent, cuts, -0.22, 0.18) if cuts else 1.0
    entries = jax.random.normal(rng, extent, jnp.float32) * scale * factor_of
    return jnp.minimum(jnp.maximum(entries, -limit), limit).astype(kind)


def setup_inputs(seed: int = 0) -> dict:
    splits = jax.random.split(jax.random.key(seed), 8)
    queries = draw_queries(jax.random.fold_in(splits[7], 71), 0)
    keys = draw_keys(jax.random.fold_in(splits[7], 71), 0)
    values = noise(splits[2], (SECTIONS, S_SEC, KV_HEADS * HEAD_DIM), 1.0, 6.0, ((0, 4), (1, 2), (2, 4)))
    seg_ids = jax.vmap(lambda own: jnp.searchsorted(jnp.cumsum(ragged_sizes(own, SEGS, S_SEC, SEG_MOST, 0)), jnp.arange(S_SEC), side="right"))(jax.random.split(splits[3], SECTIONS)).reshape((SECTIONS, S_SEC)).astype(jnp.int32)
    out_weight = noise(splits[4], (HEADS * HEAD_DIM, D), HEAD_DIM ** -0.5, 0.5, ((0, 4), (1, 2)))
    embedded = noise(splits[5], (S_SEC, D), 1.0, 6.0, ((0, 4), (1, 2)))
    hidden_prev = noise(splits[6], (SECTIONS, S_SEC, D), 1.0, 6.0, ((0, 4), (1, 4), (2, 2)))
    return {"queries": queries, "keys": keys, "values": values, "seg_ids": seg_ids, "out_weight": out_weight, "embedded": embedded, "hidden_prev": hidden_prev}


def attend(query_rows, key_rows, value_rows, segment_row):
    length = query_rows.shape[0]
    group_size = HEADS // KV_HEADS
    query_grid = query_rows.reshape(length, HEADS, HEAD_DIM)
    key_grid = key_rows.reshape(length, KV_HEADS, HEAD_DIM)
    value_grid = value_rows.reshape(length, KV_HEADS, HEAD_DIM)
    places = jnp.arange(length, dtype=jnp.int32)
    allowed = (places[:, None] >= places[None, :]) & (segment_row[:, None] == segment_row[None, :])
    score_scale = HEAD_DIM ** -0.5

    def one_head(head_index):
        kv_index = head_index // group_size
        query_head = query_grid[:, head_index, :]
        key_head = key_grid[:, kv_index, :]
        value_head = value_grid[:, kv_index, :]
        scores = jnp.dot(query_head, key_head.T, preferred_element_type=jnp.float32) * score_scale
        scores = jnp.where(allowed, scores, -1e30)
        row_max = jnp.max(scores, axis=1, keepdims=True)
        probs = jnp.where(allowed, jnp.exp(scores - row_max), 0.0)
        total = jnp.sum(probs, axis=1, keepdims=True)
        probs_low = probs.astype(jnp.bfloat16)
        return jnp.dot(probs_low, value_head, preferred_element_type=jnp.float32) / total

    heads_out = lax.map(one_head, jnp.arange(HEADS, dtype=jnp.int32))
    return jnp.transpose(heads_out, (1, 0, 2)).reshape(length, HEADS * HEAD_DIM).astype(jnp.bfloat16)


def reference(queries, keys, values, seg_ids, out_weight, embedded, hidden_prev):
    group_width = HEADS * HEAD_DIM // N_TP

    def section(section_index):
        attended = attend(queries[section_index], keys[section_index], values[section_index], seg_ids[section_index])
        branch = jnp.zeros((attended.shape[0], out_weight.shape[1]), jnp.float32)
        for group in range(N_TP):
            columns = attended[:, group * group_width:(group + 1) * group_width]
            rows = out_weight[group * group_width:(group + 1) * group_width, :]
            partial_value = jnp.dot(columns, rows, preferred_element_type=jnp.float32).astype(jnp.bfloat16)
            branch = branch + partial_value.astype(jnp.float32)
        before = hidden_prev[jnp.maximum(section_index - 1, 0)]
        resid_in = jnp.where(section_index == 0, embedded, before)
        return (resid_in.astype(jnp.float32) + branch).astype(jnp.bfloat16)

    return lax.map(section, jnp.arange(SECTIONS, dtype=jnp.int32))
```

```python
import jax
import jax.numpy as jnp
from jax import lax
from jax.experimental import pallas as pl
from jax.experimental.pallas import tpu as pltpu
from jax.sharding import PartitionSpec as P

HEAD_DIM = 128
NEG = -1e30
VMEM = pl.BlockSpec(memory_space=pltpu.VMEM)
HBM = pl.BlockSpec(memory_space=pltpu.HBM)
F32 = jnp.float32
BF16 = jnp.bfloat16


def kernel_call(body, out_shape, in_specs, scratch=(), flops=0, moved=0, mib=16):
    return pl.pallas_call(
        body,
        out_shape=out_shape,
        in_specs=in_specs,
        out_specs=jax.tree.map(lambda _: VMEM, out_shape),
        scratch_shapes=list(scratch),
        compiler_params=pltpu.CompilerParams(vmem_limit_bytes=mib * 1024 * 1024),
        cost_estimate=pl.CostEstimate(flops=flops, bytes_accessed=moved, transcendentals=0),
    )


def row_blocks(i):
    return i ^ 3, i ^ 1, i ^ 2, i


def pack(q, k, v, seg):
    rows, width = q.shape[0] // 2, q.shape[1]
    kw = k.shape[1]

    def body(q_ref, k_ref, v_ref, s_ref, x_ref, y_ref, seg_ref, sems):
        low = lax.axis_index("tp") & 1
        pieces = [(q_ref.at[pl.ds(pl.multiple_of((1 - low) * rows, rows), rows)], x_ref.at[:, 0:width])]
        at = width
        for ref in (k_ref, v_ref):
            for part in range(2):
                pieces.append((ref.at[part * rows:(part + 1) * rows], x_ref.at[:, at:at + kw]))
                at += kw
        pieces.append((q_ref.at[pl.ds(pl.multiple_of(low * rows, rows), rows)], y_ref))
        pieces.append((s_ref, seg_ref))
        copies = [pltpu.make_async_copy(a, b, sems.at[n]) for n, (a, b) in enumerate(pieces)]
        for copy in copies:
            copy.start()
        for copy in copies:
            copy.wait()

    return kernel_call(
        body,
        (
            jax.ShapeDtypeStruct((rows, width + 4 * kw), q.dtype),
            jax.ShapeDtypeStruct((rows, width), q.dtype),
            jax.ShapeDtypeStruct(seg.shape, seg.dtype),
        ),
        [HBM] * 4,
        [pltpu.SemaphoreType.DMA((7,))],
        moved=4 * q.size,
        mib=58,
    )(q, k, v, seg)


def prepare(seg, weight, rows):
    half = 2 * rows
    parts = 8

    def body(seg_ref, w_ref, wo_ref, bias_ref, col_ref, sems):
        depth = w_ref.shape[0] // parts
        copies = []
        for p in range(parts):
            at = pl.ds(p * depth, depth)
            copies.append(pltpu.make_async_copy(w_ref.at[at], wo_ref.at[at], sems.at[p]))
        for copy in copies:
            copy.start()
        c = lax.axis_index("ctx")
        seg_all = seg_ref[...].astype(F32)
        col_ref[...] = jnp.transpose(jnp.broadcast_to(seg_all, (128, 2 * half)))
        low, high = seg_all[:, :half], seg_all[:, half:]
        seg_keys = jnp.concatenate((jnp.where(c == 0, low, high), jnp.where(c == 0, high, low)), axis=1)
        column = lax.broadcasted_iota(jnp.int32, (rows, 2 * half), 1)
        key_place = jnp.where(column < half, column + c * half, column - c * half)
        for b, block in enumerate(row_blocks(lax.axis_index("tp"))):
            at = pl.multiple_of(block * rows, rows)
            row_place = lax.broadcasted_iota(jnp.int32, (rows, 2 * half), 0) + at
            allowed = (row_place >= key_place) & (col_ref[pl.ds(at, rows), 0:1] == seg_keys)
            bias_ref[b * rows:(b + 1) * rows, :] = jnp.where(allowed, 0.0, NEG)
        for copy in copies:
            copy.wait()

    return kernel_call(
        body,
        (jax.ShapeDtypeStruct(weight.shape, weight.dtype), jax.ShapeDtypeStruct((4 * rows, 2 * half), F32)),
        [VMEM, HBM],
        [pltpu.VMEM((2 * half, 128), F32), pltpu.SemaphoreType.DMA((parts,))],
        moved=weight.size * 4,
    )(seg, weight)


def keys_values(mine, other, width):
    kw = (mine.shape[1] - width) // 4

    def piece(ref, n):
        return ref[:, width + n * kw:width + (n + 1) * kw]

    k = jnp.concatenate([piece(r, n) for r in (mine, other) for n in (0, 1)], axis=0)
    v = jnp.concatenate([piece(r, n) for r in (mine, other) for n in (2, 3)], axis=0)
    return k, v


def attend(q, k, v, bias):
    rows = q.shape[0]
    heads = q.shape[1] // HEAD_DIM
    stacked = jnp.concatenate([q[:, h * HEAD_DIM:(h + 1) * HEAD_DIM] for h in range(heads)], axis=0)
    s = lax.dot_general(stacked, k, (((1,), (1,)), ((), ())), preferred_element_type=F32)
    s = (s.reshape(heads, rows, -1) + bias[None]).reshape(heads * rows, -1)
    top = jnp.max(s, axis=1, keepdims=True)
    p = jnp.exp((s - top) * (HEAD_DIM ** -0.5))
    total = jnp.sum(p, axis=1, keepdims=True)
    o = jnp.dot(p.astype(BF16), v, preferred_element_type=F32)
    o = (o / total).astype(BF16)
    return jnp.concatenate([o[h * rows:(h + 1) * rows] for h in range(heads)], axis=1)


def product(att, w_ref, at, width, store, tile=512):
    for t in range(0, width, tile):
        store(t, tile, jnp.dot(att, w_ref[:, at + t:at + t + tile], preferred_element_type=F32))


def choose(c, i, mine, other):
    return jnp.where(c == i >> 1, mine, other)


def first_block(mine, other, width, bias, weight):
    rows = mine.shape[0]
    cols = weight.shape[1] // 2

    def body(mine_ref, other_ref, bias_ref, w_ref, a0_ref, a1_ref, att_ref):
        c, i = lax.axis_index("ctx"), lax.axis_index("tp")
        q = choose(c, i, other_ref[:, :width], mine_ref[:, :width])
        k, v = keys_values(mine_ref, other_ref, width)
        att_ref[...] = attend(q, k, v, bias_ref[:rows])

        def store(t, tile, part):
            ref = a0_ref if t < cols else a1_ref
            ref[:, t % cols:t % cols + tile] = part.astype(BF16)

        product(att_ref[...], w_ref, 0, 2 * cols, store)

    out = jax.ShapeDtypeStruct((rows, cols), BF16)
    return kernel_call(
        body,
        (out, out),
        [VMEM] * 4,
        [pltpu.VMEM((rows, width), BF16)],
        flops=4 * rows * width * cols,
        moved=weight.size * 2,
    )(mine, other, bias, weight)


def add_parts(n, rows, cols, att, w_ref, at, got_ref, m_ref, f_ref, o_ref):
    def store(t, tile, part):
        m_ref[:, t:t + tile] = part[:rows].astype(BF16)
        f_ref[:, t:t + tile] = (part[rows:2 * rows] + got_ref[:, t:t + tile].astype(F32)).astype(BF16)
        o_ref[:, t:t + tile] = part[2 * rows:]

    product(att, w_ref, at, cols, store)


def other_first(mine, other, qy, ry, bias, weight, got):
    rows, width = qy.shape
    cols = weight.shape[1] // 2

    def body(mine_ref, other_ref, qy_ref, ry_ref, bias_ref, w_ref, got_ref, m_ref, f_ref, o_ref, att_ref):
        c, i = lax.axis_index("ctx"), lax.axis_index("tp")
        k, v = keys_values(mine_ref, other_ref, width)
        blocks = (
            choose(c, i, mine_ref[:, :width], other_ref[:, :width]),
            choose(c, i, ry_ref[...], qy_ref[...]),
            choose(c, i, qy_ref[...], ry_ref[...]),
        )
        for b, q in enumerate(blocks):
            att_ref[b * rows:(b + 1) * rows, :] = attend(q, k, v, bias_ref[(b + 1) * rows:(b + 2) * rows])
        add_parts(3, rows, cols, att_ref[...], w_ref, 0, got_ref, m_ref, f_ref, o_ref)

    part = jax.ShapeDtypeStruct((rows, cols), BF16)
    return kernel_call(
        body,
        (part, part, jax.ShapeDtypeStruct((rows, cols), F32), jax.ShapeDtypeStruct((3 * rows, width), BF16)),
        [VMEM] * 7,
        flops=6 * rows * width * cols,
        moved=weight.size * 2,
    )(mine, other, qy, ry, bias, weight, got)


def other_second(att, weight, got):
    rows, width = att.shape[0] // 3, att.shape[1]
    cols = weight.shape[1] // 2

    def body(att_ref, w_ref, got_ref, m_ref, f_ref, o_ref):
        add_parts(3, rows, cols, att_ref[...], w_ref, cols, got_ref, m_ref, f_ref, o_ref)

    part = jax.ShapeDtypeStruct((rows, cols), BF16)
    return kernel_call(
        body,
        (part, part, jax.ShapeDtypeStruct((rows, cols), F32)),
        [VMEM] * 3,
        flops=6 * rows * width * cols,
        moved=weight.size,
    )(att, weight, got)


def swap(x, axis, by):
    peers = lax.axis_size(axis)
    return lax.ppermute(x, axis, [(i, i ^ by) for i in range(peers)])


def after(x, *others):
    return lax.optimization_barrier((x,) + others)[0]


def passed_along(shard, axis, by):
    peers = lax.axis_size(axis)
    pairs = [(i, i + by) for i in range(peers) if 0 <= i + by < peers]
    return lax.ppermute(shard, axis, pairs)


def residual(embedded, hidden_prev):
    arrived = passed_along(hidden_prev, "phase", 1)
    return jnp.where(lax.axis_index("phase") == 0, embedded, arrived[0])


def on_pair(queries, keys, values, seg_ids, out_weight, embedded, hidden_prev):
    q = queries[0]
    rows, width = q.shape[0] // 2, q.shape[1]
    mine, qy, seg = pack(q, keys[0], values[0], seg_ids)
    other = swap(mine, "ctx", 1)
    weight, bias = prepare(seg, out_weight, rows)
    a0, a1 = first_block(mine, other, width, bias, weight)
    ry = swap(after(qy, a0), "ctx", 1)
    got0 = swap(a0, "tp", 1)
    got1 = swap(a1, "tp", 1)
    m0, f0, own0, att = other_first(mine, other, qy, ry, bias, weight, got0)
    gotm0 = swap(m0, "tp", 1)
    y0 = swap(f0, "tp", 2)
    m1, f1, own1 = other_second(att, weight, got1)
    gotm1 = swap(m1, "tp", 1)
    y1 = swap(f1, "tp", 2)
    prev = after(hidden_prev, a1)
    cols = weight.shape[1] // 2
    base0 = own0 + residual(embedded[:, :cols], prev[:, :, :cols]).astype(F32) + gotm0.astype(F32)
    base1 = own1 + residual(embedded[:, cols:], prev[:, :, cols:]).astype(F32) + gotm1.astype(F32)
    base0, base1 = lax.optimization_barrier((base0, base1, y0))[:2]
    out = jnp.concatenate((base0 + y0.astype(F32), base1 + y1.astype(F32)), axis=1)
    return out.astype(BF16)[None]


def on_device(queries, keys, values, seg_ids, out_weight, embedded, hidden_prev):
    shard_rows = queries.shape[1]
    kv_local = keys.shape[2] // HEAD_DIM
    heads_local = queries.shape[2] // HEAD_DIM
    group_size = heads_local // kv_local
    kv_width = kv_local * HEAD_DIM
    score_scale = HEAD_DIM ** (-0.5)
    ctx_place = lax.axis_index("ctx")
    offset = ctx_place * shard_rows
    query_grid = queries[0].reshape(shard_rows, kv_local, group_size, HEAD_DIM)
    segment_row = seg_ids[0]
    query_places = offset + jnp.arange(shard_rows, dtype=jnp.int32)
    query_segs = lax.dynamic_slice_in_dim(segment_row, offset, shard_rows)
    stacked = jnp.concatenate((keys, values), axis=2)
    pieces = lax.all_gather(stacked, "ctx", axis=1, tiled=True)
    length = pieces.shape[1]
    key_grid = pieces[0, :, :kv_width].reshape(length, kv_local, HEAD_DIM)
    value_grid = pieces[0, :, kv_width:].reshape(length, kv_local, HEAD_DIM)
    key_places = jnp.arange(length, dtype=jnp.int32)
    allowed = (query_places[:, None] >= key_places[None, :]) & (key_places[None, :] >= 0)
    allowed = allowed & (query_segs[:, None] == segment_row[None, :])
    mask_grid = allowed[:, None, None, :]
    scores = (
        jnp.einsum("qkgd,nkd->qkgn", query_grid, key_grid, preferred_element_type=jnp.float32)
        * score_scale
    )
    running_max = jnp.full((shard_rows, kv_local, group_size), NEG, jnp.float32)
    new_max = jnp.maximum(running_max, jnp.max(jnp.where(mask_grid, scores, NEG), axis=3))
    probs = jnp.where(mask_grid, jnp.exp(scores - new_max[..., None]), 0.0)
    new_sum = jnp.sum(probs, axis=3)
    new_out = jnp.einsum(
        "qkgn,nkd->qkgd", probs.astype(jnp.bfloat16), value_grid, preferred_element_type=jnp.float32
    )
    attended = (
        (new_out / new_sum[..., None])
        .reshape(shard_rows, heads_local * HEAD_DIM)
        .astype(jnp.bfloat16)
    )
    partial_value = jnp.dot(
        lax.all_gather(attended, "ctx", axis=0, tiled=True),
        out_weight,
        preferred_element_type=jnp.float32,
    )
    summed = lax.psum_scatter(
        partial_value.astype(jnp.bfloat16), "tp", scatter_dimension=0, tiled=True
    ).astype(jnp.float32)
    resid_in = residual(embedded, hidden_prev)
    return (resid_in.astype(jnp.float32) + summed).astype(jnp.bfloat16)[None]


def solution(mesh):
    fast = mesh.shape["ctx"] == 2 and mesh.shape["tp"] == 4
    return jax.shard_map(
        on_pair if fast else on_device,
        mesh=mesh,
        in_specs=(
            P("phase", "ctx", "tp"),
            P("phase", "ctx", "tp"),
            P("phase", "ctx", "tp"),
            P("phase", None),
            P("tp", "ctx"),
            P("tp", "ctx"),
            P("phase", "tp", "ctx"),
        ),
        out_specs=P("phase", "tp", "ctx"),
        check_vma=False,
    )
```

```python
import jax
import jax.numpy as jnp
from jax import lax
from jax.experimental import pallas as pl
from jax.experimental.pallas import tpu as pltpu
from jax.sharding import PartitionSpec as P

HEAD_DIM = 128
NEG = -1e30
VMEM = pl.BlockSpec(memory_space=pltpu.VMEM)
HBM = pl.BlockSpec(memory_space=pltpu.HBM)
F32 = jnp.float32
BF16 = jnp.bfloat16


def kernel_call(body, out_shape, in_specs, scratch=(), flops=0, moved=0, mib=16):
    return pl.pallas_call(
        body,
        out_shape=out_shape,
        in_specs=in_specs,
        out_specs=jax.tree.map(lambda _: VMEM, out_shape),
        scratch_shapes=list(scratch),
        compiler_params=pltpu.CompilerParams(vmem_limit_bytes=mib * 1024 * 1024),
        cost_estimate=pl.CostEstimate(flops=flops, bytes_accessed=moved, transcendentals=0),
    )


def row_blocks(i):
    return i ^ 3, i ^ 1, i ^ 2, i


def pack(q, k, v, seg):
    rows, width = q.shape[0] // 2, q.shape[1]
    kw = k.shape[1]

    def body(q_ref, k_ref, v_ref, s_ref, x_ref, y_ref, seg_ref, sems):
        low = lax.axis_index("tp") & 1
        pieces = [(q_ref.at[pl.ds(pl.multiple_of((1 - low) * rows, rows), rows)], x_ref.at[:, 0:width])]
        at = width
        for ref in (k_ref, v_ref):
            for part in range(2):
                pieces.append((ref.at[part * rows:(part + 1) * rows], x_ref.at[:, at:at + kw]))
                at += kw
        pieces.append((q_ref.at[pl.ds(pl.multiple_of(low * rows, rows), rows)], y_ref))
        pieces.append((s_ref, seg_ref))
        copies = [pltpu.make_async_copy(a, b, sems.at[n]) for n, (a, b) in enumerate(pieces)]
        for copy in copies:
            copy.start()
        for copy in copies:
            copy.wait()

    return kernel_call(
        body,
        (
            jax.ShapeDtypeStruct((rows, width + 4 * kw), q.dtype),
            jax.ShapeDtypeStruct((rows, width), q.dtype),
            jax.ShapeDtypeStruct(seg.shape, seg.dtype),
        ),
        [HBM] * 4,
        [pltpu.SemaphoreType.DMA((7,))],
        moved=4 * q.size,
        mib=58,
    )(q, k, v, seg)


def prepare(seg, weight, rows):
    half = 2 * rows
    parts = 8

    def body(seg_ref, w_ref, wo_ref, bias_ref, col_ref, sems):
        depth = w_ref.shape[0] // parts
        copies = []
        for p in range(parts):
            at = pl.ds(p * depth, depth)
            copies.append(pltpu.make_async_copy(w_ref.at[at], wo_ref.at[at], sems.at[p]))
        for copy in copies:
            copy.start()
        c = lax.axis_index("ctx")
        seg_all = seg_ref[...].astype(F32)
        col_ref[...] = jnp.transpose(jnp.broadcast_to(seg_all, (128, 2 * half)))
        low, high = seg_all[:, :half], seg_all[:, half:]
        seg_keys = jnp.concatenate((jnp.where(c == 0, low, high), jnp.where(c == 0, high, low)), axis=1)
        column = lax.broadcasted_iota(jnp.int32, (rows, 2 * half), 1)
        key_place = jnp.where(column < half, column + c * half, column - c * half)
        for b, block in enumerate(row_blocks(lax.axis_index("tp"))):
            at = pl.multiple_of(block * rows, rows)
            row_place = lax.broadcasted_iota(jnp.int32, (rows, 2 * half), 0) + at
            allowed = (row_place >= key_place) & (col_ref[pl.ds(at, rows), 0:1] == seg_keys)
            bias_ref[b * rows:(b + 1) * rows, :] = jnp.where(allowed, 0.0, NEG)
        for copy in copies:
            copy.wait()

    return kernel_call(
        body,
        (jax.ShapeDtypeStruct(weight.shape, weight.dtype), jax.ShapeDtypeStruct((4 * rows, 2 * half), F32)),
        [VMEM, HBM],
        [pltpu.VMEM((2 * half, 128), F32), pltpu.SemaphoreType.DMA((parts,))],
        moved=weight.size * 4,
    )(seg, weight)


def keys_values(mine, other, width):
    kw = (mine.shape[1] - width) // 4

    def piece(ref, n):
        return ref[:, width + n * kw:width + (n + 1) * kw]

    k = jnp.concatenate([piece(r, n) for r in (mine, other) for n in (0, 1)], axis=0)
    v = jnp.concatenate([piece(r, n) for r in (mine, other) for n in (2, 3)], axis=0)
    return k, v


def attend(q, k, v, bias):
    rows = q.shape[0]
    heads = q.shape[1] // HEAD_DIM
    stacked = jnp.concatenate([q[:, h * HEAD_DIM:(h + 1) * HEAD_DIM] for h in range(heads)], axis=0)
    s = lax.dot_general(stacked, k, (((1,), (1,)), ((), ())), preferred_element_type=F32)
    s = (s.reshape(heads, rows, -1) + bias[None]).reshape(heads * rows, -1)
    top = jnp.max(s, axis=1, keepdims=True)
    p = jnp.exp((s - top) * (HEAD_DIM ** -0.5))
    total = jnp.sum(p, axis=1, keepdims=True)
    o = jnp.dot(p.astype(BF16), v, preferred_element_type=F32)
    o = (o / total).astype(BF16)
    return jnp.concatenate([o[h * rows:(h + 1) * rows] for h in range(heads)], axis=1)


def product(att, w_ref, at, width, store, tile=512):
    for t in range(0, width, tile):
        store(t, tile, jnp.dot(att, w_ref[:, at + t:at + t + tile], preferred_element_type=F32))


def choose(c, i, mine, other):
    return jnp.where(c == i >> 1, mine, other)


def attend_blocks(mine, other, bias, halves=()):
    rows = mine.shape[0]
    width = mine.shape[1] - 4 * HEAD_DIM
    n = 3 if halves else 1

    def body(mine_ref, other_ref, bias_ref, *rest):
        c, i = lax.axis_index("ctx"), lax.axis_index("tp")
        att_ref = rest[-1]
        k, v = keys_values(mine_ref, other_ref, width)
        if halves:
            qy_ref, ry_ref = rest[:2]
            blocks = (
                choose(c, i, mine_ref[:, :width], other_ref[:, :width]),
                choose(c, i, ry_ref[...], qy_ref[...]),
                choose(c, i, qy_ref[...], ry_ref[...]),
            )
        else:
            blocks = (choose(c, i, other_ref[:, :width], mine_ref[:, :width]),)
        first = 1 if halves else 0
        for b, q in enumerate(blocks):
            att_ref[b * rows:(b + 1) * rows, :] = attend(q, k, v, bias_ref[(first + b) * rows:(first + b + 1) * rows])

    return kernel_call(
        body,
        jax.ShapeDtypeStruct((n * rows, width), BF16),
        [VMEM] * (3 + len(halves)),
        flops=0,
        moved=mine.size,
    )(mine, other, bias, *halves)


def first_part(att, weight, at, cols):
    rows, width = att.shape

    def body(att_ref, w_ref, a_ref):
        def store(t, tile, part):
            a_ref[:, t:t + tile] = part.astype(BF16)

        product(att_ref[...], w_ref, at, cols, store)

    return kernel_call(
        body,
        jax.ShapeDtypeStruct((rows, cols), BF16),
        [VMEM] * 2,
        flops=2 * rows * width * cols,
        moved=weight.size,
    )(att, weight)


def other_parts(att, weight, got, at):
    rows, width = att.shape[0] // 3, att.shape[1]
    cols = got.shape[1]

    def body(att_ref, w_ref, got_ref, m_ref, f_ref, o_ref):
        def store(t, tile, part):
            m_ref[:, t:t + tile] = part[:rows].astype(BF16)
            f_ref[:, t:t + tile] = (part[rows:2 * rows] + got_ref[:, t:t + tile].astype(F32)).astype(BF16)
            o_ref[:, t:t + tile] = part[2 * rows:]

        product(att_ref[...], w_ref, at, cols, store)

    part = jax.ShapeDtypeStruct((rows, cols), BF16)
    return kernel_call(
        body,
        (part, part, jax.ShapeDtypeStruct((rows, cols), F32)),
        [VMEM] * 3,
        flops=6 * rows * width * cols,
        moved=weight.size,
    )(att, weight, got)


def add_far(own, y):
    def body(o_ref, y_ref, out_ref):
        out_ref[...] = o_ref[...] + y_ref[...].astype(F32)

    return kernel_call(body, jax.ShapeDtypeStruct(own.shape, F32), [VMEM] * 2, moved=own.size * 10)(own, y)


def add_rest(sum0, own1, gotm0, y1, gotm1):
    rows, cols = sum0.shape

    def body(s_ref, o_ref, m0_ref, y_ref, m1_ref, out_ref):
        out_ref[:, :cols] = s_ref[...] + m0_ref[...].astype(F32)
        out_ref[:, cols:] = o_ref[...] + m1_ref[...].astype(F32) + y_ref[...].astype(F32)

    return kernel_call(body, jax.ShapeDtypeStruct((rows, 2 * cols), F32), [VMEM] * 5, moved=sum0.size * 22)(
        sum0, own1, gotm0, y1, gotm1
    )


def finish(branch, embedded, arrived):
    rows, cols = branch.shape
    n = len(arrived)
    step = cols // n

    def body(b_ref, e_ref, *rest):
        pieces, out_ref, done_ref, sems = rest[:n], rest[n], rest[n + 1], rest[n + 2]
        first = lax.axis_index("phase") == 0
        copies = []
        for p in range(n):
            at = slice(p * step, (p + 1) * step)
            resid = jnp.where(first, e_ref[:, at], pieces[p][...])
            done_ref[:, at] = (resid.astype(F32) + b_ref[:, at]).astype(BF16)
            copies.append(pltpu.make_async_copy(done_ref.at[:, at], out_ref.at[:, at], sems.at[p]))
            copies[-1].start()
        for copy in copies:
            copy.wait()

    return pl.pallas_call(
        body,
        out_shape=jax.ShapeDtypeStruct((rows, cols), BF16),
        in_specs=[VMEM] * (2 + n),
        out_specs=HBM,
        scratch_shapes=[pltpu.VMEM((rows, cols), BF16), pltpu.SemaphoreType.DMA((n,))],
        compiler_params=pltpu.CompilerParams(vmem_limit_bytes=16 * 1024 * 1024),
        cost_estimate=pl.CostEstimate(flops=0, bytes_accessed=branch.size * 10, transcendentals=0),
    )(branch, embedded, *arrived)


def swap(x, axis, by):
    peers = lax.axis_size(axis)
    return lax.ppermute(x, axis, [(i, i ^ by) for i in range(peers)])


def after(x, *others):
    return lax.optimization_barrier((x,) + others)[0]


def passed_along(shard, axis, by):
    peers = lax.axis_size(axis)
    pairs = [(i, i + by) for i in range(peers) if 0 <= i + by < peers]
    return lax.ppermute(shard, axis, pairs)


def residual(embedded, hidden_prev):
    arrived = passed_along(hidden_prev, "phase", 1)
    return jnp.where(lax.axis_index("phase") == 0, embedded, arrived[0])


def on_pair(queries, keys, values, seg_ids, out_weight, embedded, hidden_prev):
    q = queries[0]
    rows = q.shape[0] // 2
    cols = out_weight.shape[1] // 2
    mine, qy, seg = pack(q, keys[0], values[0], seg_ids)
    other = swap(mine, "ctx", 1)
    weight, bias = prepare(seg, out_weight, rows)
    att = attend_blocks(mine, other, bias)
    a0 = first_part(att, weight, 0, cols)
    got0 = swap(a0, "tp", 1)
    a1 = first_part(att, weight, cols, cols)
    got1 = swap(a1, "tp", 1)
    ry = swap(after(qy, a0), "ctx", 1)
    rest = attend_blocks(mine, other, bias, (qy, ry))
    m0, f0, own0 = other_parts(rest, weight, got0, 0)
    gotm0 = swap(m0, "tp", 1)
    y0 = swap(f0, "tp", 2)
    m1, f1, own1 = other_parts(rest, weight, got1, cols)
    gotm1 = swap(m1, "tp", 1)
    y1 = swap(f1, "tp", 2)
    prev = after(hidden_prev, f1)[0]
    arrived = [passed_along(prev[:, at:at + cols], "phase", 1) for at in (0, cols)]
    sum0 = add_far(own0, y0)
    branch = add_rest(sum0, own1, gotm0, y1, gotm1)
    return finish(branch, embedded, arrived)[None]


def on_device(queries, keys, values, seg_ids, out_weight, embedded, hidden_prev):
    shard_rows = queries.shape[1]
    kv_local = keys.shape[2] // HEAD_DIM
    heads_local = queries.shape[2] // HEAD_DIM
    group_size = heads_local // kv_local
    kv_width = kv_local * HEAD_DIM
    score_scale = HEAD_DIM ** (-0.5)
    ctx_place = lax.axis_index("ctx")
    offset = ctx_place * shard_rows
    query_grid = queries[0].reshape(shard_rows, kv_local, group_size, HEAD_DIM)
    segment_row = seg_ids[0]
    query_places = offset + jnp.arange(shard_rows, dtype=jnp.int32)
    query_segs = lax.dynamic_slice_in_dim(segment_row, offset, shard_rows)
    stacked = jnp.concatenate((keys, values), axis=2)
    pieces = lax.all_gather(stacked, "ctx", axis=1, tiled=True)
    length = pieces.shape[1]
    key_grid = pieces[0, :, :kv_width].reshape(length, kv_local, HEAD_DIM)
    value_grid = pieces[0, :, kv_width:].reshape(length, kv_local, HEAD_DIM)
    key_places = jnp.arange(length, dtype=jnp.int32)
    allowed = (query_places[:, None] >= key_places[None, :]) & (key_places[None, :] >= 0)
    allowed = allowed & (query_segs[:, None] == segment_row[None, :])
    mask_grid = allowed[:, None, None, :]
    scores = (
        jnp.einsum("qkgd,nkd->qkgn", query_grid, key_grid, preferred_element_type=jnp.float32)
        * score_scale
    )
    running_max = jnp.full((shard_rows, kv_local, group_size), NEG, jnp.float32)
    new_max = jnp.maximum(running_max, jnp.max(jnp.where(mask_grid, scores, NEG), axis=3))
    probs = jnp.where(mask_grid, jnp.exp(scores - new_max[..., None]), 0.0)
    new_sum = jnp.sum(probs, axis=3)
    new_out = jnp.einsum(
        "qkgn,nkd->qkgd", probs.astype(jnp.bfloat16), value_grid, preferred_element_type=jnp.float32
    )
    attended = (
        (new_out / new_sum[..., None])
        .reshape(shard_rows, heads_local * HEAD_DIM)
        .astype(jnp.bfloat16)
    )
    partial_value = jnp.dot(
        lax.all_gather(attended, "ctx", axis=0, tiled=True),
        out_weight,
        preferred_element_type=jnp.float32,
    )
    summed = lax.psum_scatter(
        partial_value.astype(jnp.bfloat16), "tp", scatter_dimension=0, tiled=True
    ).astype(jnp.float32)
    resid_in = residual(embedded, hidden_prev)
    return (resid_in.astype(jnp.float32) + summed).astype(jnp.bfloat16)[None]


def solution(mesh):
    fast = mesh.shape["ctx"] == 2 and mesh.shape["tp"] == 4
    return jax.shard_map(
        on_pair if fast else on_device,
        mesh=mesh,
        in_specs=(
            P("phase", "ctx", "tp"),
            P("phase", "ctx", "tp"),
            P("phase", "ctx", "tp"),
            P("phase", None),
            P("tp", "ctx"),
            P("tp", "ctx"),
            P("phase", "tp", "ctx"),
        ),
        out_specs=P("phase", "tp", "ctx"),
        check_vma=False,
    )
```

```python
import jax
import jax.numpy as jnp
from jax import lax
from jax.experimental import pallas as pl
from jax.experimental.pallas import tpu as pltpu
from jax.sharding import PartitionSpec as P

HEAD_DIM = 128
NEG = -1e30
VMEM = pl.BlockSpec(memory_space=pltpu.VMEM)
HBM = pl.BlockSpec(memory_space=pltpu.HBM)
F32 = jnp.float32
BF16 = jnp.bfloat16


def kernel_call(body, out_shape, in_specs, scratch=(), flops=0, moved=0, mib=16):
    return pl.pallas_call(
        body,
        out_shape=out_shape,
        in_specs=in_specs,
        out_specs=jax.tree.map(lambda _: VMEM, out_shape),
        scratch_shapes=list(scratch),
        compiler_params=pltpu.CompilerParams(vmem_limit_bytes=mib * 1024 * 1024),
        cost_estimate=pl.CostEstimate(flops=flops, bytes_accessed=moved, transcendentals=0),
    )


def row_blocks(i):
    return i ^ 3, i ^ 1, i ^ 2, i


def mask(seg, rows):
    half = 2 * rows

    def body(seg_ref, bias_ref, col_ref):
        c = lax.axis_index("ctx")
        seg_all = seg_ref[...].astype(F32)
        col_ref[...] = jnp.transpose(jnp.broadcast_to(seg_all, (128, 2 * half)))
        low, high = seg_all[:, :half], seg_all[:, half:]
        seg_keys = jnp.concatenate((jnp.where(c == 0, low, high), jnp.where(c == 0, high, low)), axis=1)
        column = lax.broadcasted_iota(jnp.int32, (rows, 2 * half), 1)
        key_place = jnp.where(column < half, column + c * half, column - c * half)
        for b, block in enumerate(row_blocks(lax.axis_index("tp"))):
            at = pl.multiple_of(block * rows, rows)
            row_place = lax.broadcasted_iota(jnp.int32, (rows, 2 * half), 0) + at
            allowed = (row_place >= key_place) & (col_ref[pl.ds(at, rows), 0:1] == seg_keys)
            bias_ref[b * rows:(b + 1) * rows, :] = jnp.where(allowed, 0.0, NEG)

    return kernel_call(
        body,
        jax.ShapeDtypeStruct((4 * rows, 2 * half), F32),
        [VMEM],
        [pltpu.VMEM((2 * half, 128), F32)],
        moved=1024,
    )(seg)


def attend(q, k, v, bias):
    rows = q.shape[0]
    heads = q.shape[1] // HEAD_DIM
    stacked = jnp.concatenate([q[:, h * HEAD_DIM:(h + 1) * HEAD_DIM] for h in range(heads)], axis=0)
    s = lax.dot_general(stacked, k, (((1,), (1,)), ((), ())), preferred_element_type=F32)
    s = (s.reshape(heads, rows, -1) + bias[None]).reshape(heads * rows, -1)
    top = jnp.max(s, axis=1, keepdims=True)
    p = jnp.exp((s - top) * (HEAD_DIM ** -0.5))
    total = jnp.sum(p, axis=1, keepdims=True)
    o = jnp.dot(p.astype(BF16), v, preferred_element_type=F32)
    o = (o / total).astype(BF16)
    return jnp.concatenate([o[h * rows:(h + 1) * rows] for h in range(heads)], axis=1)


def product(att, w_ref, store, tile=512):
    for t in range(0, w_ref.shape[1], tile):
        store(t, tile, jnp.dot(att, w_ref[:, t:t + tile], preferred_element_type=F32))


def choose(c, i, mine, other):
    return jnp.where(c == i >> 1, mine, other)


def attend_blocks(kv, bias, qx, rx, halves=()):
    rows, width = qx.shape
    n = 3 if halves else 1

    def body(kl, vl, kr, vr, bias_ref, qx_ref, rx_ref, *rest):
        c, i = lax.axis_index("ctx"), lax.axis_index("tp")
        att_ref = rest[-1]
        k = jnp.concatenate((kl[...], kr[...]), axis=0)
        v = jnp.concatenate((vl[...], vr[...]), axis=0)
        if halves:
            qy_ref, ry_ref = rest[:2]
            blocks = (
                choose(c, i, qx_ref[...], rx_ref[...]),
                choose(c, i, ry_ref[...], qy_ref[...]),
                choose(c, i, qy_ref[...], ry_ref[...]),
            )
        else:
            blocks = (choose(c, i, rx_ref[...], qx_ref[...]),)
        first = 1 if halves else 0
        for b, q in enumerate(blocks):
            att_ref[b * rows:(b + 1) * rows, :] = attend(q, k, v, bias_ref[(first + b) * rows:(first + b + 1) * rows])

    return kernel_call(
        body,
        jax.ShapeDtypeStruct((n * rows, width), BF16),
        [VMEM] * (7 + len(halves)),
        moved=qx.size * 4,
    )(*kv, bias, qx, rx, *halves)


def first_part(att, weight):
    rows, width = att.shape
    cols = weight.shape[1]

    def body(att_ref, w_ref, a_ref):
        def store(t, tile, part):
            a_ref[:, t:t + tile] = part.astype(BF16)

        product(att_ref[...], w_ref, store)

    return kernel_call(
        body,
        jax.ShapeDtypeStruct((rows, cols), BF16),
        [VMEM] * 2,
        flops=2 * rows * width * cols,
        moved=weight.size,
    )(att, weight)


def other_parts(att, weight, got):
    rows, width = att.shape[0] // 3, att.shape[1]
    cols = got.shape[1]

    def body(att_ref, w_ref, got_ref, m_ref, f_ref, o_ref):
        def store(t, tile, part):
            m_ref[:, t:t + tile] = part[:rows].astype(BF16)
            f_ref[:, t:t + tile] = (part[rows:2 * rows] + got_ref[:, t:t + tile].astype(F32)).astype(BF16)
            o_ref[:, t:t + tile] = part[2 * rows:]

        product(att_ref[...], w_ref, store)

    part = jax.ShapeDtypeStruct((rows, cols), BF16)
    return kernel_call(
        body,
        (part, part, jax.ShapeDtypeStruct((rows, cols), F32)),
        [VMEM] * 3,
        flops=6 * rows * width * cols,
        moved=weight.size,
    )(att, weight, got)


def add_far(own, y):
    def body(o_ref, y_ref, out_ref):
        out_ref[...] = o_ref[...] + y_ref[...].astype(F32)

    return kernel_call(body, jax.ShapeDtypeStruct(own.shape, F32), [VMEM] * 2, moved=own.size * 10)(own, y)


def add_rest(sum0, own1, gotm0, y1, gotm1):
    rows, cols = sum0.shape

    def body(s_ref, o_ref, m0_ref, y_ref, m1_ref, out_ref):
        out_ref[:, :cols] = s_ref[...] + m0_ref[...].astype(F32)
        out_ref[:, cols:] = o_ref[...] + m1_ref[...].astype(F32) + y_ref[...].astype(F32)

    return kernel_call(body, jax.ShapeDtypeStruct((rows, 2 * cols), F32), [VMEM] * 5, moved=sum0.size * 22)(
        sum0, own1, gotm0, y1, gotm1
    )


def finish(branch, embedded, arrived):
    rows, cols = branch.shape
    n = len(arrived)
    step = cols // n

    def body(b_ref, e_ref, *rest):
        pieces, out_ref, done_ref, sems = rest[:n], rest[n], rest[n + 1], rest[n + 2]
        first = lax.axis_index("phase") == 0
        copies = []
        for p in range(n):
            at = slice(p * step, (p + 1) * step)
            resid = jnp.where(first, e_ref[:, at], pieces[p][...])
            done_ref[:, at] = (resid.astype(F32) + b_ref[:, at]).astype(BF16)
            copies.append(pltpu.make_async_copy(done_ref.at[:, at], out_ref.at[:, at], sems.at[p]))
            copies[-1].start()
        for copy in copies:
            copy.wait()

    return pl.pallas_call(
        body,
        out_shape=jax.ShapeDtypeStruct((rows, cols), BF16),
        in_specs=[VMEM] * (2 + n),
        out_specs=HBM,
        scratch_shapes=[pltpu.VMEM((rows, cols), BF16), pltpu.SemaphoreType.DMA((n,))],
        compiler_params=pltpu.CompilerParams(vmem_limit_bytes=16 * 1024 * 1024),
        cost_estimate=pl.CostEstimate(flops=0, bytes_accessed=branch.size * 10, transcendentals=0),
    )(branch, embedded, *arrived)


def swap(x, axis, by):
    peers = lax.axis_size(axis)
    return lax.ppermute(x, axis, [(i, i ^ by) for i in range(peers)])


def after(x, *others):
    return lax.optimization_barrier((x,) + others)[0]


def passed_along(shard, axis, by):
    peers = lax.axis_size(axis)
    pairs = [(i, i + by) for i in range(peers) if 0 <= i + by < peers]
    return lax.ppermute(shard, axis, pairs)


def residual(embedded, hidden_prev):
    arrived = passed_along(hidden_prev, "phase", 1)
    return jnp.where(lax.axis_index("phase") == 0, embedded, arrived[0])


def on_pair(queries, keys, values, seg_ids, out_weight, embedded, hidden_prev):
    q = queries[0]
    rows = q.shape[0] // 2
    cols = out_weight.shape[1] // 2
    k, v = keys[0], values[0]
    kr, vr = swap(k, "ctx", 1), swap(v, "ctx", 1)
    low = lax.axis_index("tp") & 1
    qx = lax.dynamic_slice_in_dim(q, (1 - low) * rows, rows)
    qy = lax.dynamic_slice_in_dim(q, low * rows, rows)
    rx = swap(qx, "ctx", 1)
    ry = swap(qy, "ctx", 1)
    bias, left = lax.optimization_barrier((mask(seg_ids, rows), out_weight[:, :cols]))
    kv = (k, v, kr, vr)
    att = attend_blocks(kv, bias, qx, rx)
    a0 = first_part(att, left)
    got0 = swap(a0, "tp", 1)
    right = after(out_weight, a0)[:, cols:]
    rest = attend_blocks(kv, bias, qx, rx, (qy, ry))
    a1 = first_part(att, right)
    got1 = swap(a1, "tp", 1)
    m0, f0, own0 = other_parts(rest, left, got0)
    gotm0 = swap(m0, "tp", 1)
    y0 = swap(f0, "tp", 2)
    m1, f1, own1 = other_parts(rest, right, got1)
    gotm1 = swap(m1, "tp", 1)
    y1 = swap(f1, "tp", 2)
    prev = after(hidden_prev, f1)[0]
    arrived = [passed_along(prev[:, at:at + cols], "phase", 1) for at in (0, cols)]
    sum0 = add_far(own0, y0)
    branch = add_rest(sum0, own1, gotm0, y1, gotm1)
    return finish(branch, embedded, arrived)[None]


def on_device(queries, keys, values, seg_ids, out_weight, embedded, hidden_prev):
    shard_rows = queries.shape[1]
    kv_local = keys.shape[2] // HEAD_DIM
    heads_local = queries.shape[2] // HEAD_DIM
    group_size = heads_local // kv_local
    kv_width = kv_local * HEAD_DIM
    score_scale = HEAD_DIM ** (-0.5)
    ctx_place = lax.axis_index("ctx")
    offset = ctx_place * shard_rows
    query_grid = queries[0].reshape(shard_rows, kv_local, group_size, HEAD_DIM)
    segment_row = seg_ids[0]
    query_places = offset + jnp.arange(shard_rows, dtype=jnp.int32)
    query_segs = lax.dynamic_slice_in_dim(segment_row, offset, shard_rows)
    stacked = jnp.concatenate((keys, values), axis=2)
    pieces = lax.all_gather(stacked, "ctx", axis=1, tiled=True)
    length = pieces.shape[1]
    key_grid = pieces[0, :, :kv_width].reshape(length, kv_local, HEAD_DIM)
    value_grid = pieces[0, :, kv_width:].reshape(length, kv_local, HEAD_DIM)
    key_places = jnp.arange(length, dtype=jnp.int32)
    allowed = (query_places[:, None] >= key_places[None, :]) & (key_places[None, :] >= 0)
    allowed = allowed & (query_segs[:, None] == segment_row[None, :])
    mask_grid = allowed[:, None, None, :]
    scores = (
        jnp.einsum("qkgd,nkd->qkgn", query_grid, key_grid, preferred_element_type=jnp.float32)
        * score_scale
    )
    running_max = jnp.full((shard_rows, kv_local, group_size), NEG, jnp.float32)
    new_max = jnp.maximum(running_max, jnp.max(jnp.where(mask_grid, scores, NEG), axis=3))
    probs = jnp.where(mask_grid, jnp.exp(scores - new_max[..., None]), 0.0)
    new_sum = jnp.sum(probs, axis=3)
    new_out = jnp.einsum(
        "qkgn,nkd->qkgd", probs.astype(jnp.bfloat16), value_grid, preferred_element_type=jnp.float32
    )
    attended = (
        (new_out / new_sum[..., None])
        .reshape(shard_rows, heads_local * HEAD_DIM)
        .astype(jnp.bfloat16)
    )
    partial_value = jnp.dot(
        lax.all_gather(attended, "ctx", axis=0, tiled=True),
        out_weight,
        preferred_element_type=jnp.float32,
    )
    summed = lax.psum_scatter(
        partial_value.astype(jnp.bfloat16), "tp", scatter_dimension=0, tiled=True
    ).astype(jnp.float32)
    resid_in = residual(embedded, hidden_prev)
    return (resid_in.astype(jnp.float32) + summed).astype(jnp.bfloat16)[None]


def solution(mesh):
    fast = mesh.shape["ctx"] == 2 and mesh.shape["tp"] == 4
    return jax.shard_map(
        on_pair if fast else on_device,
        mesh=mesh,
        in_specs=(
            P("phase", "ctx", "tp"),
            P("phase", "ctx", "tp"),
            P("phase", "ctx", "tp"),
            P("phase", None),
            P("tp", "ctx"),
            P("tp", "ctx"),
            P("phase", "tp", "ctx"),
        ),
        out_specs=P("phase", "tp", "ctx"),
        check_vma=False,
    )
```

```python
import jax
import jax.numpy as jnp
from jax import lax
from jax.experimental import pallas as pl
from jax.experimental.pallas import tpu as pltpu
from jax.sharding import PartitionSpec as P

HEAD_DIM = 128
NEG = -1e30
HOLD = 5 * 10**9
NEAR = 4
LONG = 3 * 10**9
VMEM = pl.BlockSpec(memory_space=pltpu.VMEM)
HBM = pl.BlockSpec(memory_space=pltpu.HBM)
F32 = jnp.float32
BF16 = jnp.bfloat16


def kernel_call(body, out_shape, in_specs, scratch=(), flops=0, moved=0, mib=16):
    return pl.pallas_call(
        body,
        out_shape=out_shape,
        in_specs=in_specs,
        out_specs=jax.tree.map(lambda _: VMEM, out_shape),
        scratch_shapes=list(scratch),
        compiler_params=pltpu.CompilerParams(vmem_limit_bytes=mib * 1024 * 1024),
        cost_estimate=pl.CostEstimate(flops=flops, bytes_accessed=moved, transcendentals=0),
    )


def row_blocks(i):
    return i ^ 3, i ^ 1, i ^ 2, i


def mask(seg, rows):
    half = 2 * rows

    def body(seg_ref, bias_ref, col_ref):
        c = lax.axis_index("ctx")
        seg_all = seg_ref[...].astype(F32)
        col_ref[...] = jnp.transpose(jnp.broadcast_to(seg_all, (128, 2 * half)))
        low, high = seg_all[:, :half], seg_all[:, half:]
        seg_keys = jnp.concatenate((jnp.where(c == 0, low, high), jnp.where(c == 0, high, low)), axis=1)
        column = lax.broadcasted_iota(jnp.int32, (rows, 2 * half), 1)
        key_place = jnp.where(column < half, column + c * half, column - c * half)
        for b, block in enumerate(row_blocks(lax.axis_index("tp"))):
            at = pl.multiple_of(block * rows, rows)
            row_place = lax.broadcasted_iota(jnp.int32, (rows, 2 * half), 0) + at
            allowed = (row_place >= key_place) & (col_ref[pl.ds(at, rows), 0:1] == seg_keys)
            bias_ref[b * rows:(b + 1) * rows, :] = jnp.where(allowed, 0.0, NEG)

    return kernel_call(
        body,
        jax.ShapeDtypeStruct((4 * rows, 2 * half), F32),
        [VMEM],
        [pltpu.VMEM((2 * half, 128), F32)],
        flops=LONG,
    )(seg)


def attend(q, k, v, bias):
    rows = q.shape[0]
    heads = q.shape[1] // HEAD_DIM
    stacked = jnp.concatenate([q[:, h * HEAD_DIM:(h + 1) * HEAD_DIM] for h in range(heads)], axis=0)
    s = lax.dot_general(stacked, k, (((1,), (1,)), ((), ())), preferred_element_type=F32)
    s = (s.reshape(heads, rows, -1) + bias[None]).reshape(heads * rows, -1)
    top = jnp.max(s, axis=1, keepdims=True)
    p = jnp.exp((s - top) * (HEAD_DIM ** -0.5))
    total = jnp.sum(p, axis=1, keepdims=True)
    o = jnp.dot(p.astype(BF16), v, preferred_element_type=F32)
    o = (o / total).astype(BF16)
    return jnp.concatenate([o[h * rows:(h + 1) * rows] for h in range(heads)], axis=1)


def product(att, w_ref, at, cols, store, tile=512):
    for t in range(0, cols, tile):
        store(t, tile, jnp.dot(att, w_ref[:, at + t:at + t + tile], preferred_element_type=F32))


def choose(c, i, mine, other):
    return jnp.where(c == i >> 1, mine, other)


def attend_blocks(kv, bias, qx, rx, halves=()):
    rows, width = qx.shape
    n = 3 if halves else 1

    def body(kl, vl, kr, vr, bias_ref, qx_ref, rx_ref, *rest):
        c, i = lax.axis_index("ctx"), lax.axis_index("tp")
        att_ref = rest[-1]
        k = jnp.concatenate((kl[...], kr[...]), axis=0)
        v = jnp.concatenate((vl[...], vr[...]), axis=0)
        if halves:
            qy_ref, ry_ref = rest[:2]
            blocks = (
                choose(c, i, qx_ref[...], rx_ref[...]),
                choose(c, i, ry_ref[...], qy_ref[...]),
                choose(c, i, qy_ref[...], ry_ref[...]),
            )
        else:
            blocks = (choose(c, i, rx_ref[...], qx_ref[...]),)
        first = 1 if halves else 0
        for b, q in enumerate(blocks):
            att_ref[b * rows:(b + 1) * rows, :] = attend(q, k, v, bias_ref[(first + b) * rows:(first + b + 1) * rows])

    return kernel_call(
        body,
        jax.ShapeDtypeStruct((n * rows, width), BF16),
        [VMEM] * (7 + len(halves)),
        moved=qx.size * 4,
    )(*kv, bias, qx, rx, *halves)


def first_part(att, weight, at, cols):
    rows, width = att.shape

    def body(att_ref, w_ref, a_ref):
        def store(t, tile, part):
            a_ref[:, t:t + tile] = part.astype(BF16)

        product(att_ref[...], w_ref, at, cols, store)

    return kernel_call(
        body,
        jax.ShapeDtypeStruct((rows, cols), BF16),
        [VMEM] * 2,
        flops=2 * rows * width * cols,
        moved=weight.size,
    )(att, weight)


def other_parts(att, weight, at, got, hint):
    rows, width = att.shape[0] // 3, att.shape[1]
    cols = got.shape[1]

    def body(att_ref, w_ref, got_ref, m_ref, f_ref, o_ref):
        def store(t, tile, part):
            m_ref[:, t:t + tile] = part[:rows].astype(BF16)
            f_ref[:, t:t + tile] = (part[rows:2 * rows] + got_ref[:, t:t + tile].astype(F32)).astype(BF16)
            o_ref[:, t:t + tile] = part[2 * rows:]

        product(att_ref[...], w_ref, at, cols, store)

    part = jax.ShapeDtypeStruct((rows, cols), BF16)
    return kernel_call(
        body,
        (part, part, jax.ShapeDtypeStruct((rows, cols), F32)),
        [VMEM] * 3,
        flops=hint,
        moved=weight.size,
    )(att, weight, got)


def add_far(own, y):
    def body(o_ref, y_ref, out_ref):
        out_ref[...] = o_ref[...] + y_ref[...].astype(F32)

    return kernel_call(body, jax.ShapeDtypeStruct(own.shape, F32), [VMEM] * 2, moved=own.size * 10)(own, y)


def finish(parts, embedded, arrived, at, out, hint):
    rows, cols = arrived.shape
    n = len(parts)

    def body(*refs):
        e_ref, a_ref = refs[n:n + 2]
        out_ref, done_ref, sem = refs[-3:]
        resid = jnp.where(lax.axis_index("phase") == 0, e_ref[:, at:at + cols], a_ref[...])
        total = resid.astype(F32)
        for ref in refs[:n]:
            total = total + ref[...].astype(F32)
        done_ref[...] = total.astype(BF16)
        copy = pltpu.make_async_copy(done_ref, out_ref.at[:, at:at + cols], sem)
        copy.start()
        copy.wait()

    before = () if out is None else (out,)
    return pl.pallas_call(
        body,
        out_shape=jax.ShapeDtypeStruct(embedded.shape, BF16),
        in_specs=[VMEM] * (n + 2) + [HBM] * len(before),
        out_specs=HBM,
        scratch_shapes=[pltpu.VMEM((rows, cols), BF16), pltpu.SemaphoreType.DMA],
        input_output_aliases={n + 2: 0} if before else {},
        compiler_params=pltpu.CompilerParams(vmem_limit_bytes=16 * 1024 * 1024),
        cost_estimate=pl.CostEstimate(flops=hint, bytes_accessed=embedded.size * 4, transcendentals=0),
    )(*parts, embedded, arrived, *before)


def swap(x, axis, by):
    peers = lax.axis_size(axis)
    return lax.ppermute(x, axis, [(i, i ^ by) for i in range(peers)])


def after(x, *others):
    return lax.optimization_barrier((x,) + others)[0]


def passed_along(shard, axis, by):
    peers = lax.axis_size(axis)
    pairs = [(i, i + by) for i in range(peers) if 0 <= i + by < peers]
    return lax.ppermute(shard, axis, pairs)


def residual(embedded, hidden_prev):
    arrived = passed_along(hidden_prev, "phase", 1)
    return jnp.where(lax.axis_index("phase") == 0, embedded, arrived[0])


def on_pair(queries, keys, values, seg_ids, out_weight, embedded, hidden_prev):
    q = queries[0]
    rows = q.shape[0] // 2
    cols = out_weight.shape[1] // 2
    near = NEAR * cols // 4
    k, v = keys[0], values[0]
    low = lax.axis_index("tp") & 1
    qx = lax.dynamic_slice_in_dim(q, (1 - low) * rows, rows)
    qy = lax.dynamic_slice_in_dim(q, low * rows, rows)
    rx = swap(qx, "ctx", 1)
    kr, vr = swap(after(k, qx), "ctx", 1), swap(after(v, qx), "ctx", 1)
    bias = mask(seg_ids, rows)
    kv = (k, v, kr, vr)
    att = attend_blocks(kv, bias, qx, rx)
    a0 = first_part(att, out_weight, 0, near)
    got0 = swap(a0, "tp", 1)
    ry = swap(after(qy, a0), "ctx", 1)
    a1 = first_part(after(att, a0), out_weight, near, 2 * cols - near)
    got1 = swap(a1, "tp", 1)
    rest = attend_blocks(kv, bias, qx, rx, (qy, ry))
    m0, f0, own0 = other_parts(rest, out_weight, 0, got0, HOLD)
    gotm0 = swap(m0, "tp", 1)
    y0 = swap(f0, "tp", 2)
    m1, f1, own1 = other_parts(rest, out_weight, near, got1, 0)
    gotm1 = swap(m1, "tp", 1)
    y1 = swap(f1, "tp", 2)
    prev = after(hidden_prev, f1)[0]
    arrived = [passed_along(prev[:, at:at + cols], "phase", 1) for at in (0, cols)]
    sum0 = add_far(own0, y0)
    out = finish((sum0, gotm0), embedded, arrived[0], 0, None, 0)
    return finish((own1, y1, gotm1), embedded, arrived[1], cols, out, 0)[None]


def on_device(queries, keys, values, seg_ids, out_weight, embedded, hidden_prev):
    shard_rows = queries.shape[1]
    kv_local = keys.shape[2] // HEAD_DIM
    heads_local = queries.shape[2] // HEAD_DIM
    group_size = heads_local // kv_local
    kv_width = kv_local * HEAD_DIM
    score_scale = HEAD_DIM ** (-0.5)
    ctx_place = lax.axis_index("ctx")
    offset = ctx_place * shard_rows
    query_grid = queries[0].reshape(shard_rows, kv_local, group_size, HEAD_DIM)
    segment_row = seg_ids[0]
    query_places = offset + jnp.arange(shard_rows, dtype=jnp.int32)
    query_segs = lax.dynamic_slice_in_dim(segment_row, offset, shard_rows)
    stacked = jnp.concatenate((keys, values), axis=2)
    pieces = lax.all_gather(stacked, "ctx", axis=1, tiled=True)
    length = pieces.shape[1]
    key_grid = pieces[0, :, :kv_width].reshape(length, kv_local, HEAD_DIM)
    value_grid = pieces[0, :, kv_width:].reshape(length, kv_local, HEAD_DIM)
    key_places = jnp.arange(length, dtype=jnp.int32)
    allowed = (query_places[:, None] >= key_places[None, :]) & (key_places[None, :] >= 0)
    allowed = allowed & (query_segs[:, None] == segment_row[None, :])
    mask_grid = allowed[:, None, None, :]
    scores = (
        jnp.einsum("qkgd,nkd->qkgn", query_grid, key_grid, preferred_element_type=jnp.float32)
        * score_scale
    )
    running_max = jnp.full((shard_rows, kv_local, group_size), NEG, jnp.float32)
    new_max = jnp.maximum(running_max, jnp.max(jnp.where(mask_grid, scores, NEG), axis=3))
    probs = jnp.where(mask_grid, jnp.exp(scores - new_max[..., None]), 0.0)
    new_sum = jnp.sum(probs, axis=3)
    new_out = jnp.einsum(
        "qkgn,nkd->qkgd", probs.astype(jnp.bfloat16), value_grid, preferred_element_type=jnp.float32
    )
    attended = (
        (new_out / new_sum[..., None])
        .reshape(shard_rows, heads_local * HEAD_DIM)
        .astype(jnp.bfloat16)
    )
    partial_value = jnp.dot(
        lax.all_gather(attended, "ctx", axis=0, tiled=True),
        out_weight,
        preferred_element_type=jnp.float32,
    )
    summed = lax.psum_scatter(
        partial_value.astype(jnp.bfloat16), "tp", scatter_dimension=0, tiled=True
    ).astype(jnp.float32)
    resid_in = residual(embedded, hidden_prev)
    return (resid_in.astype(jnp.float32) + summed).astype(jnp.bfloat16)[None]


def solution(mesh):
    fast = mesh.shape["ctx"] == 2 and mesh.shape["tp"] == 4
    return jax.shard_map(
        on_pair if fast else on_device,
        mesh=mesh,
        in_specs=(
            P("phase", "ctx", "tp"),
            P("phase", "ctx", "tp"),
            P("phase", "ctx", "tp"),
            P("phase", None),
            P("tp", "ctx"),
            P("tp", "ctx"),
            P("phase", "tp", "ctx"),
        ),
        out_specs=P("phase", "tp", "ctx"),
        check_vma=False,
    )
```

```python
import jax
import jax.numpy as jnp
from jax import lax
from jax.experimental import pallas as pl
from jax.experimental.pallas import tpu as pltpu
from jax.sharding import PartitionSpec as P

HEAD_DIM = 128
NEG = -1e30
LONG = 3 * 10**9
HOLD = 5 * 10**9
VMEM = pl.BlockSpec(memory_space=pltpu.VMEM)
HBM = pl.BlockSpec(memory_space=pltpu.HBM)
F32 = jnp.float32
BF16 = jnp.bfloat16


def kernel_call(body, out_shape, in_specs, scratch=(), flops=0, moved=0, mib=16):
    return pl.pallas_call(
        body,
        out_shape=out_shape,
        in_specs=in_specs,
        out_specs=jax.tree.map(lambda _: VMEM, out_shape),
        scratch_shapes=list(scratch),
        compiler_params=pltpu.CompilerParams(vmem_limit_bytes=mib * 1024 * 1024),
        cost_estimate=pl.CostEstimate(flops=flops, bytes_accessed=moved, transcendentals=0),
    )


def row_blocks(i):
    return i ^ 3, i ^ 1, i ^ 2, i


def mask(seg, rows):
    half = 2 * rows

    def body(seg_ref, bias_ref, col_ref):
        c = lax.axis_index("ctx")
        seg_all = seg_ref[...].astype(F32)
        col_ref[...] = jnp.transpose(jnp.broadcast_to(seg_all, (128, 2 * half)))
        low, high = seg_all[:, :half], seg_all[:, half:]
        seg_keys = jnp.concatenate((jnp.where(c == 0, low, high), jnp.where(c == 0, high, low)), axis=1)
        column = lax.broadcasted_iota(jnp.int32, (rows, 2 * half), 1)
        key_place = jnp.where(column < half, column + c * half, column - c * half)
        for b, block in enumerate(row_blocks(lax.axis_index("tp"))):
            at = pl.multiple_of(block * rows, rows)
            row_place = lax.broadcasted_iota(jnp.int32, (rows, 2 * half), 0) + at
            allowed = (row_place >= key_place) & (col_ref[pl.ds(at, rows), 0:1] == seg_keys)
            bias_ref[b * rows:(b + 1) * rows, :] = jnp.where(allowed, 0.0, NEG)

    return kernel_call(
        body,
        jax.ShapeDtypeStruct((4 * rows, 2 * half), F32),
        [VMEM],
        [pltpu.VMEM((2 * half, 128), F32)],
        flops=LONG,
    )(seg)


def attend(q, k, v, bias):
    rows = q.shape[0]
    heads = q.shape[1] // HEAD_DIM
    stacked = jnp.concatenate([q[:, h * HEAD_DIM:(h + 1) * HEAD_DIM] for h in range(heads)], axis=0)
    s = lax.dot_general(stacked, k, (((1,), (1,)), ((), ())), preferred_element_type=F32)
    s = (s.reshape(heads, rows, -1) + bias[None]).reshape(heads * rows, -1)
    top = jnp.max(s, axis=1, keepdims=True)
    p = jnp.exp((s - top) * (HEAD_DIM ** -0.5))
    total = jnp.sum(p, axis=1, keepdims=True)
    o = jnp.dot(p.astype(BF16), v, preferred_element_type=F32)
    o = (o / total).astype(BF16)
    return jnp.concatenate([o[h * rows:(h + 1) * rows] for h in range(heads)], axis=1)


def product(att, w_ref, at, cols, store, tile=512):
    for t in range(0, cols, tile):
        store(t, tile, jnp.dot(att, w_ref[:, at + t:at + t + tile], preferred_element_type=F32))


def choose(c, i, mine, other):
    return jnp.where(c == i >> 1, mine, other)


def other_blocks(kv, bias, qx, rx, qy, ry):
    rows, width = qx.shape

    def body(kl, vl, kr, vr, bias_ref, qx_ref, rx_ref, qy_ref, ry_ref, att_ref):
        c, i = lax.axis_index("ctx"), lax.axis_index("tp")
        k = jnp.concatenate((kl[...], kr[...]), axis=0)
        v = jnp.concatenate((vl[...], vr[...]), axis=0)
        blocks = (
            choose(c, i, qx_ref[...], rx_ref[...]),
            choose(c, i, ry_ref[...], qy_ref[...]),
            choose(c, i, qy_ref[...], ry_ref[...]),
        )
        for b, q in enumerate(blocks):
            att_ref[b * rows:(b + 1) * rows, :] = attend(q, k, v, bias_ref[(b + 1) * rows:(b + 2) * rows])

    return kernel_call(
        body,
        jax.ShapeDtypeStruct((3 * rows, width), BF16),
        [VMEM] * 9,
        moved=qx.size * 4,
    )(*kv, bias, qx, rx, qy, ry)


def first_block(kv, bias, qx, rx, weight, cols):
    rows, width = qx.shape

    def body(kl, vl, kr, vr, bias_ref, qx_ref, rx_ref, w_ref, a_ref, att_ref):
        c, i = lax.axis_index("ctx"), lax.axis_index("tp")
        k = jnp.concatenate((kl[...], kr[...]), axis=0)
        v = jnp.concatenate((vl[...], vr[...]), axis=0)
        att_ref[...] = attend(choose(c, i, rx_ref[...], qx_ref[...]), k, v, bias_ref[:rows])

        def store(t, tile, part):
            a_ref[:, t:t + tile] = part.astype(BF16)

        product(att_ref[...], w_ref, 0, cols, store)

    return kernel_call(
        body,
        (jax.ShapeDtypeStruct((rows, cols), BF16), jax.ShapeDtypeStruct((rows, width), BF16)),
        [VMEM] * 8,
        flops=2 * rows * width * cols,
        moved=weight.size,
    )(*kv, bias, qx, rx, weight)


def first_part(att, weight, at, cols):
    rows, width = att.shape

    def body(att_ref, w_ref, a_ref):
        def store(t, tile, part):
            a_ref[:, t:t + tile] = part.astype(BF16)

        product(att_ref[...], w_ref, at, cols, store)

    return kernel_call(
        body,
        jax.ShapeDtypeStruct((rows, cols), BF16),
        [VMEM] * 2,
        flops=2 * rows * width * cols,
        moved=weight.size,
    )(att, weight)


def other_parts(att, weight, at, got, hint):
    rows, width = att.shape[0] // 3, att.shape[1]
    cols = got.shape[1]

    def body(att_ref, w_ref, got_ref, m_ref, f_ref, o_ref):
        def store(t, tile, part):
            m_ref[:, t:t + tile] = part[:rows].astype(BF16)
            f_ref[:, t:t + tile] = (part[rows:2 * rows] + got_ref[:, t:t + tile].astype(F32)).astype(BF16)
            o_ref[:, t:t + tile] = part[2 * rows:]

        product(att_ref[...], w_ref, at, cols, store)

    part = jax.ShapeDtypeStruct((rows, cols), BF16)
    return kernel_call(
        body,
        (part, part, jax.ShapeDtypeStruct((rows, cols), F32)),
        [VMEM] * 3,
        flops=hint,
        moved=weight.size,
    )(att, weight, got)


def add_far(own, y):
    def body(o_ref, y_ref, out_ref):
        out_ref[...] = o_ref[...] + y_ref[...].astype(F32)

    return kernel_call(body, jax.ShapeDtypeStruct(own.shape, F32), [VMEM] * 2, moved=own.size * 10)(own, y)


def finish(parts, embedded, arrived, at, out):
    rows, cols = arrived.shape
    n = len(parts)
    step = cols // 2

    def body(*refs):
        e_ref, a_ref = refs[n:n + 2]
        out_ref, done_ref, sems = refs[-3:]
        first = lax.axis_index("phase") == 0
        copies = []
        for p in range(2):
            a, b = p * step, (p + 1) * step
            total = jnp.where(first, e_ref[:, at + a:at + b], a_ref[:, a:b]).astype(F32)
            for ref in refs[:n]:
                total = total + ref[:, a:b].astype(F32)
            done_ref[:, a:b] = total.astype(BF16)
            copies.append(pltpu.make_async_copy(done_ref.at[:, a:b], out_ref.at[:, at + a:at + b], sems.at[p]))
            copies[-1].start()
        for copy in copies:
            copy.wait()

    before = () if out is None else (out,)
    return pl.pallas_call(
        body,
        out_shape=jax.ShapeDtypeStruct(embedded.shape, BF16),
        in_specs=[VMEM] * (n + 2) + [HBM] * len(before),
        out_specs=HBM,
        scratch_shapes=[pltpu.VMEM((rows, cols), BF16), pltpu.SemaphoreType.DMA((2,))],
        input_output_aliases={n + 2: 0} if before else {},
        compiler_params=pltpu.CompilerParams(vmem_limit_bytes=16 * 1024 * 1024),
        cost_estimate=pl.CostEstimate(flops=0, bytes_accessed=embedded.size * 4, transcendentals=0),
    )(*parts, embedded, arrived, *before)


def swap(x, axis, by):
    peers = lax.axis_size(axis)
    return lax.ppermute(x, axis, [(i, i ^ by) for i in range(peers)])


def after(x, *others):
    return lax.optimization_barrier((x,) + others)[0]


def passed_along(shard, axis, by):
    peers = lax.axis_size(axis)
    pairs = [(i, i + by) for i in range(peers) if 0 <= i + by < peers]
    return lax.ppermute(shard, axis, pairs)


def residual(embedded, hidden_prev):
    arrived = passed_along(hidden_prev, "phase", 1)
    return jnp.where(lax.axis_index("phase") == 0, embedded, arrived[0])


def on_pair(queries, keys, values, seg_ids, out_weight, embedded, hidden_prev):
    q = queries[0]
    rows = q.shape[0] // 2
    cols = out_weight.shape[1] // 2
    k, v = keys[0], values[0]
    low = lax.axis_index("tp") & 1
    qx = lax.dynamic_slice_in_dim(q, (1 - low) * rows, rows)
    qy = lax.dynamic_slice_in_dim(q, low * rows, rows)
    rx = swap(qx, "ctx", 1)
    kr, vr = swap(after(k, qx), "ctx", 1), swap(after(v, qx), "ctx", 1)
    bias = mask(seg_ids, rows)
    kv = (k, v, kr, vr)
    a0, att = first_block(kv, bias, qx, rx, out_weight, cols)
    got0 = swap(a0, "tp", 1)
    ry = swap(after(qy, a0), "ctx", 1)
    a1 = first_part(after(att, a0), out_weight, cols, cols)
    got1 = swap(a1, "tp", 1)
    rest = other_blocks(kv, bias, qx, rx, qy, ry)
    m0, f0, own0 = other_parts(rest, out_weight, 0, got0, HOLD)
    gotm0 = swap(m0, "tp", 1)
    y0 = swap(f0, "tp", 2)
    m1, f1, own1 = other_parts(rest, out_weight, cols, got1, 0)
    gotm1 = swap(m1, "tp", 1)
    y1 = swap(f1, "tp", 2)
    prev = after(hidden_prev, f1)[0]
    arrived = [passed_along(prev[:, at:at + cols], "phase", 1) for at in (0, cols)]
    sum0 = add_far(own0, y0)
    out = finish((sum0, gotm0), embedded, arrived[0], 0, None)
    return finish((own1, y1, gotm1), embedded, arrived[1], cols, out)[None]


def on_device(queries, keys, values, seg_ids, out_weight, embedded, hidden_prev):
    shard_rows = queries.shape[1]
    kv_local = keys.shape[2] // HEAD_DIM
    heads_local = queries.shape[2] // HEAD_DIM
    group_size = heads_local // kv_local
    kv_width = kv_local * HEAD_DIM
    score_scale = HEAD_DIM ** (-0.5)
    ctx_place = lax.axis_index("ctx")
    offset = ctx_place * shard_rows
    query_grid = queries[0].reshape(shard_rows, kv_local, group_size, HEAD_DIM)
    segment_row = seg_ids[0]
    query_places = offset + jnp.arange(shard_rows, dtype=jnp.int32)
    query_segs = lax.dynamic_slice_in_dim(segment_row, offset, shard_rows)
    stacked = jnp.concatenate((keys, values), axis=2)
    pieces = lax.all_gather(stacked, "ctx", axis=1, tiled=True)
    length = pieces.shape[1]
    key_grid = pieces[0, :, :kv_width].reshape(length, kv_local, HEAD_DIM)
    value_grid = pieces[0, :, kv_width:].reshape(length, kv_local, HEAD_DIM)
    key_places = jnp.arange(length, dtype=jnp.int32)
    allowed = (query_places[:, None] >= key_places[None, :]) & (key_places[None, :] >= 0)
    allowed = allowed & (query_segs[:, None] == segment_row[None, :])
    mask_grid = allowed[:, None, None, :]
    scores = (
        jnp.einsum("qkgd,nkd->qkgn", query_grid, key_grid, preferred_element_type=jnp.float32)
        * score_scale
    )
    running_max = jnp.full((shard_rows, kv_local, group_size), NEG, jnp.float32)
    new_max = jnp.maximum(running_max, jnp.max(jnp.where(mask_grid, scores, NEG), axis=3))
    probs = jnp.where(mask_grid, jnp.exp(scores - new_max[..., None]), 0.0)
    new_sum = jnp.sum(probs, axis=3)
    new_out = jnp.einsum(
        "qkgn,nkd->qkgd", probs.astype(jnp.bfloat16), value_grid, preferred_element_type=jnp.float32
    )
    attended = (
        (new_out / new_sum[..., None])
        .reshape(shard_rows, heads_local * HEAD_DIM)
        .astype(jnp.bfloat16)
    )
    partial_value = jnp.dot(
        lax.all_gather(attended, "ctx", axis=0, tiled=True),
        out_weight,
        preferred_element_type=jnp.float32,
    )
    summed = lax.psum_scatter(
        partial_value.astype(jnp.bfloat16), "tp", scatter_dimension=0, tiled=True
    ).astype(jnp.float32)
    resid_in = residual(embedded, hidden_prev)
    return (resid_in.astype(jnp.float32) + summed).astype(jnp.bfloat16)[None]


def on_any(queries, keys, *rest):
    pair = lax.axis_size("ctx") == 2 and lax.axis_size("tp") == 4 and keys.shape[2] == HEAD_DIM
    return (on_pair if pair else on_device)(queries, keys, *rest)


def solution(mesh):
    return jax.shard_map(
        on_any,
        mesh=mesh,
        in_specs=(
            P("phase", "ctx", "tp"),
            P("phase", "ctx", "tp"),
            P("phase", "ctx", "tp"),
            P("phase", None),
            P("tp", "ctx"),
            P("tp", "ctx"),
            P("phase", "tp", "ctx"),
        ),
        out_specs=P("phase", "tp", "ctx"),
        check_vma=False,
    )
```

```python
import jax
import jax.numpy as jnp
from jax import lax
from jax.experimental import pallas as pl
from jax.experimental.pallas import tpu as pltpu
from jax.sharding import PartitionSpec as P

HEAD_DIM = 128
NEG = -1e30
LONG = 6 * 10**9
HOLD = 5 * 10**9
VMEM = pl.BlockSpec(memory_space=pltpu.VMEM)
HBM = pl.BlockSpec(memory_space=pltpu.HBM)
F32 = jnp.float32
BF16 = jnp.bfloat16


def kernel_call(body, out_shape, in_specs, scratch=(), flops=0, moved=0, mib=16):
    return pl.pallas_call(
        body,
        out_shape=out_shape,
        in_specs=in_specs,
        out_specs=jax.tree.map(lambda _: VMEM, out_shape),
        scratch_shapes=list(scratch),
        compiler_params=pltpu.CompilerParams(vmem_limit_bytes=mib * 1024 * 1024),
        cost_estimate=pl.CostEstimate(flops=flops, bytes_accessed=moved, transcendentals=0),
    )


def row_blocks(i):
    return i ^ 3, i ^ 1, i ^ 2, i


def mask(seg, rows):
    half = 2 * rows

    def body(seg_ref, bias_ref, col_ref):
        c = lax.axis_index("ctx")
        seg_all = seg_ref[...].astype(F32)
        col_ref[...] = jnp.transpose(jnp.broadcast_to(seg_all, (128, 2 * half)))
        low, high = seg_all[:, :half], seg_all[:, half:]
        seg_keys = jnp.concatenate((jnp.where(c == 0, low, high), jnp.where(c == 0, high, low)), axis=1)
        column = lax.broadcasted_iota(jnp.int32, (rows, 2 * half), 1)
        key_place = jnp.where(column < half, column + c * half, column - c * half)
        for b, block in enumerate(row_blocks(lax.axis_index("tp"))):
            at = pl.multiple_of(block * rows, rows)
            row_place = lax.broadcasted_iota(jnp.int32, (rows, 2 * half), 0) + at
            allowed = (row_place >= key_place) & (col_ref[pl.ds(at, rows), 0:1] == seg_keys)
            bias_ref[b * rows:(b + 1) * rows, :] = jnp.where(allowed, 0.0, NEG)

    return kernel_call(
        body,
        jax.ShapeDtypeStruct((4 * rows, 2 * half), F32),
        [VMEM],
        [pltpu.VMEM((2 * half, 128), F32)],
        flops=LONG,
    )(seg)


def attend(q, k, v, bias):
    rows = q.shape[0]
    heads = q.shape[1] // HEAD_DIM
    stacked = jnp.concatenate([q[:, h * HEAD_DIM:(h + 1) * HEAD_DIM] for h in range(heads)], axis=0)
    s = lax.dot_general(stacked, k, (((1,), (1,)), ((), ())), preferred_element_type=F32)
    s = (s.reshape(heads, rows, -1) + bias[None]).reshape(heads * rows, -1)
    top = jnp.max(s, axis=1, keepdims=True)
    p = jnp.exp((s - top) * (HEAD_DIM ** -0.5))
    total = jnp.sum(p, axis=1, keepdims=True)
    o = jnp.dot(p.astype(BF16), v, preferred_element_type=F32)
    o = (o / total).astype(BF16)
    return jnp.concatenate([o[h * rows:(h + 1) * rows] for h in range(heads)], axis=1)


def product(att, w_ref, at, cols, store, tile=512):
    for t in range(0, cols, tile):
        store(t, tile, jnp.dot(att, w_ref[:, at + t:at + t + tile], preferred_element_type=F32))


def choose(c, i, mine, other):
    return jnp.where(c == i >> 1, mine, other)


def other_blocks(kv, bias, qx, rx, qy, ry):
    rows, width = qx.shape

    def body(kl, vl, kr, vr, bias_ref, qx_ref, rx_ref, qy_ref, ry_ref, att_ref):
        c, i = lax.axis_index("ctx"), lax.axis_index("tp")
        k = jnp.concatenate((kl[...], kr[...]), axis=0)
        v = jnp.concatenate((vl[...], vr[...]), axis=0)
        blocks = (
            choose(c, i, qx_ref[...], rx_ref[...]),
            choose(c, i, ry_ref[...], qy_ref[...]),
            choose(c, i, qy_ref[...], ry_ref[...]),
        )
        for b, q in enumerate(blocks):
            att_ref[b * rows:(b + 1) * rows, :] = attend(q, k, v, bias_ref[(b + 1) * rows:(b + 2) * rows])

    return kernel_call(
        body,
        jax.ShapeDtypeStruct((3 * rows, width), BF16),
        [VMEM] * 9,
        moved=qx.size * 4,
    )(*kv, bias, qx, rx, qy, ry)


def first_block(kv, bias, qx, rx, weight, cols):
    rows, width = qx.shape

    def body(kl, vl, kr, vr, bias_ref, qx_ref, rx_ref, w_ref, a_ref, att_ref):
        c, i = lax.axis_index("ctx"), lax.axis_index("tp")
        k = jnp.concatenate((kl[...], kr[...]), axis=0)
        v = jnp.concatenate((vl[...], vr[...]), axis=0)
        att_ref[...] = attend(choose(c, i, rx_ref[...], qx_ref[...]), k, v, bias_ref[:rows])

        def store(t, tile, part):
            a_ref[:, t:t + tile] = part.astype(BF16)

        product(att_ref[...], w_ref, 0, cols, store)

    return kernel_call(
        body,
        (jax.ShapeDtypeStruct((rows, cols), BF16), jax.ShapeDtypeStruct((rows, width), BF16)),
        [VMEM] * 8,
        flops=2 * rows * width * cols,
        moved=weight.size,
    )(*kv, bias, qx, rx, weight)


def first_part(att, weight, at, cols):
    rows, width = att.shape

    def body(att_ref, w_ref, a_ref):
        def store(t, tile, part):
            a_ref[:, t:t + tile] = part.astype(BF16)

        product(att_ref[...], w_ref, at, cols, store)

    return kernel_call(
        body,
        jax.ShapeDtypeStruct((rows, cols), BF16),
        [VMEM] * 2,
        flops=2 * rows * width * cols,
        moved=weight.size,
    )(att, weight)


def other_parts(att, weight, at, got, hint):
    rows, width = att.shape[0] // 3, att.shape[1]
    cols = got.shape[1]

    def body(att_ref, w_ref, got_ref, m_ref, f_ref, o_ref):
        def store(t, tile, part):
            m_ref[:, t:t + tile] = part[:rows].astype(BF16)
            f_ref[:, t:t + tile] = (part[rows:2 * rows] + got_ref[:, t:t + tile].astype(F32)).astype(BF16)
            o_ref[:, t:t + tile] = part[2 * rows:]

        product(att_ref[...], w_ref, at, cols, store)

    part = jax.ShapeDtypeStruct((rows, cols), BF16)
    return kernel_call(
        body,
        (part, part, jax.ShapeDtypeStruct((rows, cols), F32)),
        [VMEM] * 3,
        flops=hint,
        moved=weight.size,
    )(att, weight, got)


def add_far(own, y):
    def body(o_ref, y_ref, out_ref):
        out_ref[...] = o_ref[...] + y_ref[...].astype(F32)

    return kernel_call(body, jax.ShapeDtypeStruct(own.shape, F32), [VMEM] * 2, moved=own.size * 10)(own, y)


def finish(parts, embedded, arrived, at, out):
    rows, cols = arrived.shape
    n = len(parts)
    step = cols // 2

    def body(*refs):
        e_ref, a_ref = refs[n:n + 2]
        out_ref, done_ref, sems = refs[-3:]
        first = lax.axis_index("phase") == 0
        copies = []
        for p in range(2):
            a, b = p * step, (p + 1) * step
            total = jnp.where(first, e_ref[:, at + a:at + b], a_ref[:, a:b]).astype(F32)
            for ref in refs[:n]:
                total = total + ref[:, a:b].astype(F32)
            done_ref[:, a:b] = total.astype(BF16)
            copies.append(pltpu.make_async_copy(done_ref.at[:, a:b], out_ref.at[:, at + a:at + b], sems.at[p]))
            copies[-1].start()
        for copy in copies:
            copy.wait()

    before = () if out is None else (out,)
    return pl.pallas_call(
        body,
        out_shape=jax.ShapeDtypeStruct(embedded.shape, BF16),
        in_specs=[VMEM] * (n + 2) + [HBM] * len(before),
        out_specs=HBM,
        scratch_shapes=[pltpu.VMEM((rows, cols), BF16), pltpu.SemaphoreType.DMA((2,))],
        input_output_aliases={n + 2: 0} if before else {},
        compiler_params=pltpu.CompilerParams(vmem_limit_bytes=16 * 1024 * 1024),
        cost_estimate=pl.CostEstimate(flops=0, bytes_accessed=embedded.size * 4, transcendentals=0),
    )(*parts, embedded, arrived, *before)


def swap(x, axis, by):
    peers = lax.axis_size(axis)
    return lax.ppermute(x, axis, [(i, i ^ by) for i in range(peers)])


def after(x, *others):
    return lax.optimization_barrier((x,) + others)[0]


def passed_along(shard, axis, by):
    peers = lax.axis_size(axis)
    pairs = [(i, i + by) for i in range(peers) if 0 <= i + by < peers]
    return lax.ppermute(shard, axis, pairs)


def residual(embedded, hidden_prev):
    arrived = passed_along(hidden_prev, "phase", 1)
    return jnp.where(lax.axis_index("phase") == 0, embedded, arrived[0])


def on_pair(queries, keys, values, seg_ids, out_weight, embedded, hidden_prev):
    q = queries[0]
    rows = q.shape[0] // 2
    cols = out_weight.shape[1] // 2
    k, v = keys[0], values[0]
    low = lax.axis_index("tp") & 1
    qx = lax.dynamic_slice_in_dim(q, (1 - low) * rows, rows)
    qy = lax.dynamic_slice_in_dim(q, low * rows, rows)
    rx = swap(qx, "ctx", 1)
    kr, vr = swap(after(k, qx), "ctx", 1), swap(after(v, qx), "ctx", 1)
    bias = mask(seg_ids, rows)
    kv = (k, v, kr, vr)
    a0, att = first_block(kv, bias, qx, rx, out_weight, cols)
    got0 = swap(a0, "tp", 1)
    ry = swap(after(qy, a0), "ctx", 1)
    a1 = first_part(after(att, a0), out_weight, cols, cols)
    got1 = swap(a1, "tp", 1)
    rest = other_blocks(kv, bias, qx, rx, qy, ry)
    m0, f0, own0 = other_parts(rest, out_weight, 0, got0, HOLD)
    gotm0 = swap(m0, "tp", 1)
    y0 = swap(f0, "tp", 2)
    m1, f1, own1 = other_parts(rest, out_weight, cols, got1, 0)
    gotm1 = swap(m1, "tp", 1)
    y1 = swap(f1, "tp", 2)
    prev = after(hidden_prev, f1)[0]
    arrived = [passed_along(prev[:, at:at + cols], "phase", 1) for at in (0, cols)]
    sum0 = add_far(own0, y0)
    out = finish((sum0, gotm0), embedded, arrived[0], 0, None)
    return finish((own1, y1, gotm1), embedded, arrived[1], cols, out)[None]


def on_device(queries, keys, values, seg_ids, out_weight, embedded, hidden_prev):
    shard_rows = queries.shape[1]
    kv_local = keys.shape[2] // HEAD_DIM
    heads_local = queries.shape[2] // HEAD_DIM
    group_size = heads_local // kv_local
    kv_width = kv_local * HEAD_DIM
    score_scale = HEAD_DIM ** (-0.5)
    ctx_place = lax.axis_index("ctx")
    offset = ctx_place * shard_rows
    query_grid = queries[0].reshape(shard_rows, kv_local, group_size, HEAD_DIM)
    segment_row = seg_ids[0]
    query_places = offset + jnp.arange(shard_rows, dtype=jnp.int32)
    query_segs = lax.dynamic_slice_in_dim(segment_row, offset, shard_rows)
    stacked = jnp.concatenate((keys, values), axis=2)
    pieces = lax.all_gather(stacked, "ctx", axis=1, tiled=True)
    length = pieces.shape[1]
    key_grid = pieces[0, :, :kv_width].reshape(length, kv_local, HEAD_DIM)
    value_grid = pieces[0, :, kv_width:].reshape(length, kv_local, HEAD_DIM)
    key_places = jnp.arange(length, dtype=jnp.int32)
    allowed = (query_places[:, None] >= key_places[None, :]) & (key_places[None, :] >= 0)
    allowed = allowed & (query_segs[:, None] == segment_row[None, :])
    mask_grid = allowed[:, None, None, :]
    scores = (
        jnp.einsum("qkgd,nkd->qkgn", query_grid, key_grid, preferred_element_type=jnp.float32)
        * score_scale
    )
    running_max = jnp.full((shard_rows, kv_local, group_size), NEG, jnp.float32)
    new_max = jnp.maximum(running_max, jnp.max(jnp.where(mask_grid, scores, NEG), axis=3))
    probs = jnp.where(mask_grid, jnp.exp(scores - new_max[..., None]), 0.0)
    new_sum = jnp.sum(probs, axis=3)
    new_out = jnp.einsum(
        "qkgn,nkd->qkgd", probs.astype(jnp.bfloat16), value_grid, preferred_element_type=jnp.float32
    )
    attended = (
        (new_out / new_sum[..., None])
        .reshape(shard_rows, heads_local * HEAD_DIM)
        .astype(jnp.bfloat16)
    )
    partial_value = jnp.dot(
        lax.all_gather(attended, "ctx", axis=0, tiled=True),
        out_weight,
        preferred_element_type=jnp.float32,
    )
    summed = lax.psum_scatter(
        partial_value.astype(jnp.bfloat16), "tp", scatter_dimension=0, tiled=True
    ).astype(jnp.float32)
    resid_in = residual(embedded, hidden_prev)
    return (resid_in.astype(jnp.float32) + summed).astype(jnp.bfloat16)[None]


def on_any(queries, keys, *rest):
    pair = lax.axis_size("ctx") == 2 and lax.axis_size("tp") == 4 and keys.shape[2] == HEAD_DIM
    return (on_pair if pair else on_device)(queries, keys, *rest)


def solution(mesh):
    return jax.shard_map(
        on_any,
        mesh=mesh,
        in_specs=(
            P("phase", "ctx", "tp"),
            P("phase", "ctx", "tp"),
            P("phase", "ctx", "tp"),
            P("phase", None),
            P("tp", "ctx"),
            P("tp", "ctx"),
            P("phase", "tp", "ctx"),
        ),
        out_specs=P("phase", "tp", "ctx"),
        check_vma=False,
    )
```
